256 devices in a mesh: row: 32 (over z, x_lo, core), col: 8 (over x_hi, y).
Axes of the slice: x: 4 (x_hi: 2, x_lo: 2; x = x_hi * 2 + x_lo), y: 4, z: 8, core: 2. Of those that a mesh axis runs over, the one named last changes fastest.
Arguments:
- images: bfloat16 [16384, 1152], P(('row', 'col')), may hold values from -8 to 8
- texts: bfloat16 [16384, 1152], P(('row', 'col')), may hold values from -8 to 8
- log_scale: float32 [1], replicated, may hold values from 1.8 to 3
- bias: float32 [1], replicated, may hold values from -12 to -6
Outputs:
- image_grad: float32 [16384, 1152], P(('row', 'col'))
- text_grad: float32 [16384, 1152], P(('row', 'col'))
- loss: float32 [1], replicated
- log_scale_grad: float32 [1], replicated
- bias_grad: float32 [1], replicated
The draws below stay inside these ranges and needn't reach their ends.
All inputs are finite; a program needn't handle non-finite values.
Results may differ from the reference program's by a relative error of at most 0.002.
The reference program's roundings to bfloat16 on the way (of `image_half` and `weighted`) count: a program that leaves them out, or rounds other values in their place, can miss the bound.
Values may be sent and summed in bfloat16 or wider, within the bound.
A program may use at most 64 MiB of HBM per device.

```python
import math
import jax
import jax.numpy as jnp
from jax import lax

D = 1152
PAIRS = 16384


def shared_parts(key):
    base = jax.random.normal(jax.random.fold_in(key, 11), (PAIRS, D), jnp.float32)
    return base


def noisy_copy(key, base):
    noise = jax.random.normal(jax.random.fold_in(key, 21), (PAIRS, D), jnp.float32)
    values = base + 0.8 * noise
    return jnp.clip(values, -8.0, 8.0).astype(jnp.bfloat16)


def draw_images(key, part):
    base = shared_parts(key)
    key = jax.random.fold_in(key, 1)
    return noisy_copy(key, base)


def draw_texts(key, part):
    base = shared_parts(key)
    key = jax.random.fold_in(key, 2)
    return noisy_copy(key, base)


def setup_inputs(seed: int = 0) -> dict:
    arg_keys = jax.random.split(jax.random.key(seed), 5)
    images = draw_images(jax.random.fold_in(arg_keys[4], 71), 0)
    texts = draw_texts(jax.random.fold_in(arg_keys[4], 71), 0)
    log_scale = jnp.clip(jax.random.uniform(arg_keys[2], (1,), jnp.float32, 1.8, 3.0), 1.8, 3.0)
    bias = jnp.clip(jax.random.uniform(arg_keys[3], (1,), jnp.float32, -12.0, -6.0), -12.0, -6.0)
    return {"images": images, "texts": texts, "log_scale": log_scale, "bias": bias}


def unit_rows(raw):
    values = raw.astype(jnp.float32)
    inverse = lax.rsqrt(lax.optimization_barrier(jnp.sum(values * values, axis=1, keepdims=True)) + 1e-06)
    return (values * inverse, inverse)

def back_rows(unit, inverse, grad):
    return inverse * (grad - unit * lax.optimization_barrier(jnp.sum(unit * grad, axis=1, keepdims=True)))

def reference(images, texts, log_scale, bias):
    image_unit, image_inv = unit_rows(images)
    text_unit, text_inv = unit_rows(texts)
    image_half = image_unit.astype(jnp.bfloat16)
    text_half = text_unit.astype(jnp.bfloat16)
    total = images.shape[0]
    block_rows = math.gcd(total, 512)
    scale = jnp.exp(log_scale[0])
    shift = bias[0]
    indices = jnp.arange(total, dtype=jnp.int32)
    starts = jnp.arange(0, total, block_rows, dtype=jnp.int32)

    def advance(totals, offset):
        text_acc, stats = totals
        rows_half = lax.dynamic_slice_in_dim(image_half, offset, block_rows, 0)
        cosine = lax.dot_general(rows_half, text_half, (((1,), (1,)), ((), ())), preferred_element_type=jnp.float32)
        same = (offset + jnp.arange(block_rows, dtype=jnp.int32))[:, None] == indices[None, :]
        sign = jnp.where(same, jnp.float32(1.0), jnp.float32(-1.0))
        logit = scale * cosine + shift
        loss_sum = jnp.sum(jax.nn.softplus(-sign * logit))
        dlogit = -sign * jax.nn.sigmoid(-sign * logit) / total
        weighted = (scale * dlogit).astype(jnp.bfloat16)
        image_part = jnp.dot(weighted, text_half, preferred_element_type=jnp.float32)
        text_acc = text_acc + lax.dot_general(weighted, rows_half, (((0,), (0,)), ((), ())), preferred_element_type=jnp.float32)
        stats = stats + jnp.stack([loss_sum, jnp.sum(dlogit * scale * cosine), jnp.sum(dlogit)])
        return ((text_acc, stats), image_part)
    init = (jnp.zeros(texts.shape, jnp.float32), jnp.zeros((3,), jnp.float32))
    (text_ugrad, stats), image_parts = lax.scan(advance, init, starts)
    image_ugrad = image_parts.reshape(images.shape)
    image_grad = back_rows(image_unit, image_inv, image_ugrad)
    text_grad = back_rows(text_unit, text_inv, text_ugrad)
    return (image_grad, text_grad, stats[0:1] / total, stats[1:2], stats[2:3])
```

```python
import jax
import jax.numpy as jnp
from jax import lax
from jax.experimental import pallas as pl
from jax.experimental.pallas import tpu as pltpu
from jax.sharding import PartitionSpec as P

MESH = pl.DeviceIdType.MESH
F32 = jnp.float32
BF16 = jnp.bfloat16
ROWS = 64
QUARTER = 16
HALF = 32
WIDTH = 1152
PAIRS = 16384
TILE = 1024

GATHER_PARTS = (
    ((0, 1),),
    ((0, 1), (1, 2)),
    ((0, 1), (1, 2), (2, 4)),
    ((0, 1), (1, 2), (2, 4), (4, 8)),
)
REDUCE_PARTS = (
    ((1, 2),),
    ((3, 4), (2, 3)),
    ((6, 8), (5, 6), (4, 5)),
    ((12, 16), (10, 12), (9, 10), (8, 9)),
)
FIRST_PART = (0, 1, 3, 6)
UP = {0: 0, 1: 2, 2: 4, 3: 6, 4: 7}
DOWN = {0: 0, 1: 1, 2: 3, 3: 5, 4: 7}


def encode(v):
    squared = v * v
    return (v * jnp.abs(v) * squared).astype(BF16)


def decode(y):
    y = y.astype(F32)
    root = lax.rsqrt(lax.rsqrt(jnp.maximum(jnp.abs(y), 1e-37)))
    return jnp.where(y > 0.0, root, jnp.where(y < 0.0, -root, 0.0))


def kernel(
    images, texts, log_scale, bias,
    image_grad, text_grad, loss_out, scale_out, bias_out,
    img, txt, cos, w, wt, iacc, tacc, isend, irecv, csend, crecv, tsend, trecv, stat, acc,
    gi_s, gi_r, gt_s, gt_r, gc_s, gc_r, ri_s, ri_r, rc_s, rc_r, rt_s, rt_r, st_s, st_r,
):
    row = lax.axis_index("row")
    col = lax.axis_index("col")
    x = 2 * (col // 4) + (row // 2) % 2
    y = col % 4
    z = row // 4
    core = row % 2

    def device(x, y, z, core):
        return (z * 4 + (x % 2) * 2 + core, (x // 2) * 4 + y)

    x_flip = x + 1 - 2 * (x % 2)
    y_flip = y + 1 - 2 * (y % 2)
    plane = (
        device(x_flip, y, z, core),
        device(x, y_flip, z, core),
        device(3 - x, y, z, core),
        device(x, 3 - y, z, core),
    )
    above = device(x, y, (z + 1) % 8, core)
    below = device(x, y, (z + 7) % 8, core)
    sibling = device(x, y, z, 1 - core)

    barrier = pltpu.get_barrier_semaphore()
    for other in (*plane, above, below, sibling):
        pl.semaphore_signal(barrier, inc=1, device_id=other, device_id_type=MESH)

    sent = []

    def copy(src, dst, send, recv, to):
        return pltpu.make_async_remote_copy(
            src_ref=src, dst_ref=dst, send_sem=send, recv_sem=recv, device_id=to, device_id_type=MESH
        )

    def start(c):
        c.start()
        sent.append(c)

    def gather_image(q, s, part):
        a, b = GATHER_PARTS[s][part]
        n = FIRST_PART[s] + part
        return copy(
            img.at[a:b, q], img.at[2**s + a : 2**s + b, q], gi_s.at[q, n], gi_r.at[q, n], plane[(q + s) % 4]
        )

    def gather_text(way, step, half):
        slots = (UP, DOWN)[way]
        src, dst = slots[step], slots[step + 1]
        rows = slice(half * HALF, (half + 1) * HALF)
        return copy(
            txt.at[src, 0, rows], txt.at[dst, 0, rows],
            gt_s.at[way, step, half], gt_r.at[way, step, half], (above, below)[way],
        )

    def share_text(slot, half):
        rows = slice(half * HALF, (half + 1) * HALF)
        return copy(txt.at[slot, 0, rows], txt.at[slot, 1, rows], gc_s.at[slot, half], gc_r.at[slot, half], sibling)

    def reduce_image(q, s, part):
        a, b = REDUCE_PARTS[s][part]
        n = FIRST_PART[s] + part
        return copy(isend.at[a:b, q], irecv.at[a:b, q], ri_s.at[q, n], ri_r.at[q, n], plane[(q + s) % 4])

    def share_sum(slot):
        return copy(csend.at[slot], crecv.at[slot], rc_s.at[slot], rc_r.at[slot], sibling)

    def reduce_text(way, m, half):
        rows = slice(half * HALF, (half + 1) * HALF)
        return copy(
            tsend.at[way, m, rows], trecv.at[way, m, rows],
            rt_s.at[way, m, half], rt_r.at[way, m, half], (above, below)[way],
        )

    def send_stat(n, src, to):
        return copy(stat.at[src], stat.at[n], st_s.at[n], st_r.at[n], to)

    def unit_rows(raw):
        values = raw[...].astype(F32)
        inverse = lax.rsqrt(jnp.sum(values * values, axis=1, keepdims=True) + 1e-06)
        return values * inverse, inverse

    img[0] = unit_rows(images)[0].astype(BF16).reshape(4, QUARTER, WIDTH)
    txt[0, 0] = unit_rows(texts)[0].astype(BF16)
    scale = jnp.exp(jnp.full((1, 128), log_scale[0], F32))
    shift = bias[0]
    acc[...] = jnp.zeros_like(acc)
    pl.semaphore_wait(barrier, 7)

    def squash(first_row, first_col, columns):
        groups = [
            range(a, min(a + 4, columns // 128)) for a in range(0, columns // 128, 4)
        ]

        def strip(i, sums):
            loss, scaled, plain = sums
            at = pl.multiple_of(i * 16, 16)
            for group in groups:
                joint = None
                for j in group:
                    c = cos[pl.ds(at, 16), j * 128 : (j + 1) * 128]
                    sc = c * scale
                    e = jnp.exp(sc + shift)
                    gate = e / (1.0 + e)
                    w[pl.ds(pl.multiple_of(first_row + i * 16, 16), 16), first_col + j * 128 : first_col + (j + 1) * 128] = (
                        scale * gate
                    ).astype(BF16)
                    joint = e if joint is None else joint + e + joint * e
                    scaled = scaled + gate * sc
                    plain = plain + gate
                loss = loss + jnp.log1p(joint)
            return loss, scaled, plain

        sums = lax.fori_loop(0, 16, strip, (acc[0], acc[1], acc[2]))
        for k in range(3):
            acc[k] = sums[k]

    def tile(first_slot, end_slot, first_text, end_text):
        columns = (end_text - first_text) * 128
        first_col = first_text * 128

        def part(i, _):
            slot = first_slot + i * 4
            cos[:, :columns] = lax.dot_general(
                img[pl.ds(slot, 4)].reshape(256, WIDTH),
                txt[first_text:end_text].reshape(columns, WIDTH),
                (((1,), (1,)), ((), ())),
                preferred_element_type=F32,
            )
            first_row = pl.multiple_of(slot * 64, 256)
            squash(first_row, first_col, columns)
            wt[first_col : first_col + columns, pl.ds(first_row, 256)] = w[
                pl.ds(first_row, 256), first_col : first_col + columns
            ].T
            return 0

        lax.fori_loop(0, (end_slot - first_slot) // 4, part, 0)

    def own_pairs():
        c = cos[:ROWS, :128]
        sc = c * scale
        logit = sc + shift
        same = lax.broadcasted_iota(jnp.int32, (ROWS, 128), 0) == lax.broadcasted_iota(jnp.int32, (ROWS, 128), 1)
        fixed = jnp.where(same, -scale / (1.0 + jnp.exp(logit)), w[:ROWS, :128].astype(F32))
        w[:ROWS, :128] = fixed.astype(BF16)
        wt[:128, :128] = w[:128, :128].T
        for k, v in enumerate((logit, sc, jnp.ones_like(sc))):
            acc[k] = acc[k] - jnp.where(same, v, 0.0).reshape(4, 16, 128).sum(axis=0)

    for s in range(4):
        for q in range(4):
            start(gather_image(q, s, 0))
        if s < 2:
            for way in range(2):
                start(gather_text(way, 0, s if way == 0 else 1 - s))
    for half in range(2):
        start(share_text(0, half))

    def pass_text(way, step, half):
        gather_text(way, step, half).wait_recv()
        slot = (UP, DOWN)[way][step + 1]
        if step < 2 or (step == 2 and half == way):
            start(gather_text(way, step + 1, half))
        start(share_text(slot, half))

    def got_image(s, part):
        for q in range(4):
            gather_image(q, s, part).wait_recv()

    def pass_image(stages, part):
        for s in stages:
            for q in range(4):
                start(gather_image(q, s, part))

    def got_shared(slots):
        for slot in slots:
            for half in range(2):
                share_text(slot, half).wait_recv()

    got_image(0, 0)
    pass_image((1, 2, 3), 1)
    for way in range(2):
        pass_text(way, 0, way)
    got_image(1, 0)
    got_image(1, 1)
    pass_image((2, 3), 2)
    for way in range(2):
        pass_text(way, 0, 1 - way)
    got_shared((0, 1, 2))
    tile(0, 4, 0, 3)
    own_pairs()
    for way in range(2):
        pass_text(way, 1, way)
    for way in range(2):
        pass_text(way, 1, 1 - way)
    for part in range(3):
        got_image(2, part)
    pass_image((3,), 3)
    got_shared((3, 4))
    tile(0, 4, 3, 5)
    for way in range(2):
        pass_text(way, 2, way)
    tile(4, 8, 0, 5)
    for way in range(2):
        pass_text(way, 2, 1 - way)
    for part in range(3):
        got_image(3, part)
    tile(8, 12, 0, 5)
    for way in range(2):
        pass_text(way, 3, way)
    got_shared((5, 6, 7))
    tile(0, 12, 5, 8)
    got_image(3, 3)
    tile(12, 16, 0, 8)

    stat[0] = jnp.zeros((8, 128), F32)
    for k in range(3):
        stat[0, k : k + 1] = jnp.sum(acc[k], axis=0, keepdims=True)
    start(send_stat(1, 0, sibling))

    def stat_chip():
        send_stat(1, 0, sibling).wait_recv()
        stat[2] = stat[0] + stat[1]
        start(send_stat(3, 2, above))
        start(send_stat(7, 2, below))

    def stat_ring(step):
        send_stat(2 + step, 2, above).wait_recv()
        if step < 4:
            send_stat(6 + step, 2, below).wait_recv()
            start(send_stat(3 + step, 2 + step, above))
        if step < 3:
            start(send_stat(7 + step, 6 + step, below))
        if step == 4:
            total = stat[2]
            for n in range(3, 10):
                total = total + stat[n]
            stat[10] = total
            start(send_stat(11, 10, plane[0]))

    def stat_plane(stage):
        n = 10 + 2 * stage
        send_stat(n + 1, n, plane[stage]).wait_recv()
        stat[n + 2] = stat[n] + stat[n + 1]
        if stage < 3:
            start(send_stat(n + 3, n + 2, plane[stage + 1]))

    def image_part(slot):
        return jnp.dot(
            w[slot * 64 : (slot + 4) * 64, :], txt[...].reshape(TILE, WIDTH), preferred_element_type=F32
        ).reshape(4, 4, QUARTER, WIDTH)

    def text_part(slot, count):
        part = jnp.dot(
            wt[slot * 128 : (slot + count) * 128, :], img[...].reshape(TILE, WIDTH), preferred_element_type=F32
        ).reshape(count, 2, ROWS, WIDTH)
        csend[slot : slot + count] = encode(part[:, 1])
        tacc[slot : slot + count] = part[:, 0]
        for k in range(slot, slot + count):
            start(share_sum(k))

    def send_images(s, parts):
        for part in parts:
            for q in range(4):
                start(reduce_image(q, s, part))

    def wait_images(s, part):
        for q in range(4):
            reduce_image(q, s, part).wait_recv()

    def add_images(first, count, stage, forward):
        def one(i, _):
            slot, q = first + i // 4, i % 4
            total = iacc[slot, q] + decode(irecv[2**stage + slot, q])
            if forward:
                isend[slot, q] = encode(total)
            else:
                iacc[slot, q] = total
            return 0

        lax.fori_loop(0, 4 * count, one, 0)

    def join_texts(slot):
        share_sum(slot).wait_recv()

        def one(i, _):
            rows = pl.ds(pl.multiple_of(i * 16, 16), 16)
            tacc[slot, rows] = tacc[slot, rows] + decode(crecv[slot, rows])
            return 0

        lax.fori_loop(0, 4, one, 0)

    def pass_sum(way, m, half):
        slot = (DOWN, UP)[way][m]
        arrives = m == 3 and half == way or m < 3
        if arrives:
            reduce_text(way, m + 1, half).wait_recv()
        for i in range(2):
            rows = slice(half * HALF + i * 16, half * HALF + (i + 1) * 16)
            total = tacc[slot, rows]
            if arrives:
                total = total + decode(trecv[way, m + 1, rows])
            tsend[way, m, rows] = encode(total)
        start(reduce_text(way, m, half))

    text_part(7, 1)
    isend[12:16] = encode(image_part(12))
    send_images(3, (0,))
    join_texts(7)
    for way in range(2):
        pass_sum(way, 4, way)
    text_part(5, 2)
    stat_chip()
    isend[8:12] = encode(image_part(8))
    send_images(3, (1, 2, 3))
    join_texts(5)
    join_texts(6)
    for way in range(2):
        pass_sum(way, 3, 1 - way)
    text_part(3, 2)
    stat_ring(1)
    iacc[4:8] = image_part(4)
    for way in range(2):
        pass_sum(way, 3, way)
    join_texts(3)
    join_texts(4)
    stat_ring(2)
    for way in range(2):
        pass_sum(way, 2, 1 - way)
    wait_images(3, 0)
    add_images(4, 4, 3, True)
    send_images(2, (0, 1, 2))
    iacc[0:4] = image_part(0)
    text_part(0, 3)
    stat_ring(3)
    for way in range(2):
        pass_sum(way, 2, way)
    for slot in (0, 1, 2):
        join_texts(slot)
    for way in range(2):
        pass_sum(way, 1, 1 - way)
    for part in (1, 2, 3):
        wait_images(3, part)
    add_images(0, 4, 3, False)
    stat_ring(4)
    wait_images(2, 0)
    add_images(2, 2, 2, True)
    send_images(1, (0, 1))
    for way in range(2):
        pass_sum(way, 1, way)
    stat_plane(0)
    wait_images(2, 1)
    wait_images(2, 2)
    add_images(0, 2, 2, False)
    stat_plane(1)
    wait_images(1, 0)
    add_images(1, 1, 1, True)
    send_images(0, (0,))
    stat_plane(2)
    wait_images(1, 1)
    add_images(0, 1, 1, False)

    def back_rows(raw, grad):
        unit, inverse = unit_rows(raw)
        grad = grad * (1.0 / PAIRS)
        return inverse * (grad - unit * jnp.sum(unit * grad, axis=1, keepdims=True))

    for way in range(2):
        for half in range(2):
            reduce_text(way, 1, half).wait_recv()
    text_grad[...] = back_rows(texts, tacc[0] + decode(trecv[0, 1]) + decode(trecv[1, 1]))
    stat_plane(3)
    wait_images(0, 0)
    image_grad[...] = back_rows(images, (iacc[0] + decode(irecv[1])).reshape(ROWS, WIDTH))
    loss_out[0] = jnp.sum(stat[18, 0:1]) * (1.0 / PAIRS)
    scale_out[0] = jnp.sum(stat[18, 1:2]) * (1.0 / PAIRS)
    bias_out[0] = jnp.sum(stat[18, 2:3]) * (1.0 / PAIRS)
    for c in sent:
        c.wait_send()


def body(images, texts, log_scale, bias):
    vmem = pl.BlockSpec(memory_space=pltpu.VMEM)
    smem = pl.BlockSpec(memory_space=pltpu.SMEM)
    dma = pltpu.SemaphoreType.DMA
    grad = jax.ShapeDtypeStruct((ROWS, WIDTH), F32)
    scalar = jax.ShapeDtypeStruct((1,), F32)
    return pl.pallas_call(
        kernel,
        out_shape=(grad, grad, scalar, scalar, scalar),
        in_specs=[vmem, vmem, smem, smem],
        out_specs=(vmem, vmem, smem, smem, smem),
        scratch_shapes=[
            pltpu.VMEM((16, 4, QUARTER, WIDTH), BF16),
            pltpu.VMEM((8, 2, ROWS, WIDTH), BF16),
            pltpu.VMEM((256, TILE), F32),
            pltpu.VMEM((TILE, TILE), BF16),
            pltpu.VMEM((TILE, TILE), BF16),
            pltpu.VMEM((8, 4, QUARTER, WIDTH), F32),
            pltpu.VMEM((8, ROWS, WIDTH), F32),
            pltpu.VMEM((16, 4, QUARTER, WIDTH), BF16),
            pltpu.VMEM((16, 4, QUARTER, WIDTH), BF16),
            pltpu.VMEM((8, ROWS, WIDTH), BF16),
            pltpu.VMEM((8, ROWS, WIDTH), BF16),
            pltpu.VMEM((2, 5, ROWS, WIDTH), BF16),
            pltpu.VMEM((2, 5, ROWS, WIDTH), BF16),
            pltpu.VMEM((19, 8, 128), F32),
            pltpu.VMEM((3, 16, 128), F32),
            dma((4, 10)), dma((4, 10)),
            dma((2, 4, 2)), dma((2, 4, 2)),
            dma((8, 2)), dma((8, 2)),
            dma((4, 10)), dma((4, 10)),
            dma((8,)), dma((8,)),
            dma((2, 5, 2)), dma((2, 5, 2)),
            dma((19,)), dma((19,)),
        ],
        compiler_params=pltpu.CompilerParams(
            collective_id=0, has_side_effects=True, vmem_limit_bytes=56 * 2**20
        ),
        cost_estimate=pl.CostEstimate(flops=6 * TILE * TILE * WIDTH, bytes_accessed=2**20, transcendentals=2 * TILE * TILE),
        name="pairs",
    )(images, texts, log_scale, bias)


def solution(mesh):
    rows = P(("row", "col"), None)
    return jax.shard_map(
        body,
        mesh=mesh,
        in_specs=(rows, rows, P(), P()),
        out_specs=(rows, rows, P(), P(), P()),
        check_vma=False,
    )
```

```python
import jax
import jax.numpy as jnp
from jax import lax
from jax.experimental import pallas as pl
from jax.experimental.pallas import tpu as pltpu
from jax.sharding import PartitionSpec as P

MESH = pl.DeviceIdType.MESH
F32 = jnp.float32
BF16 = jnp.bfloat16
ROWS = 64
QUARTER = 16
HALF = 32
WIDTH = 1152
PAIRS = 16384
LOG2E = 1.4426950408889634
TILE = 1024

GATHER_PARTS = (
    ((0, 1),),
    ((0, 1), (1, 2)),
    ((0, 1), (1, 2), (2, 4)),
    ((0, 1), (1, 2), (2, 4), (4, 8)),
)
REDUCE_PARTS = (
    ((1, 2),),
    ((3, 4), (2, 3)),
    ((6, 8), (5, 6), (4, 5)),
    ((12, 16), (10, 12), (9, 10), (8, 9)),
)
FIRST_PART = (0, 1, 3, 6)
UP = {0: 0, 1: 2, 2: 4, 3: 6, 4: 7}
DOWN = {0: 0, 1: 1, 2: 3, 3: 5, 4: 7}


def unit_rows(raw):
    values = raw[...].astype(F32)
    inverse = lax.rsqrt(jnp.sum(values * values, axis=1, keepdims=True) + 1e-06)
    return values * inverse, inverse


def encode(v):
    squared = v * v
    return (v * jnp.abs(v) * squared).astype(BF16)


def decode(y):
    y = y.astype(F32)
    root = lax.rsqrt(lax.rsqrt(jnp.maximum(jnp.abs(y), 1e-37)))
    return jnp.where(y > 0.0, root, jnp.where(y < 0.0, -root, 0.0))


def kernel(
    images_in, texts_in, log_scale, bias,
    image_sum, text_sum, stat_sum,
    img, txt, w, iacc, tacc, isend, irecv, csend, crecv, tsend, trecv, stat, acc,
    gi_s, gi_r, gt_s, gt_r, gc_s, gc_r, ri_s, ri_r, rc_s, rc_r, rt_s, rt_r, st_s, st_r, images, texts, in_s,
):
    row = lax.axis_index("row")
    col = lax.axis_index("col")
    x = 2 * (col // 4) + (row // 2) % 2
    y = col % 4
    z = row // 4
    core = row % 2

    def device(x, y, z, core):
        return (z * 4 + (x % 2) * 2 + core, (x // 2) * 4 + y)

    x_flip = x + 1 - 2 * (x % 2)
    y_flip = y + 1 - 2 * (y % 2)
    plane = (
        device(x_flip, y, z, core),
        device(x, y_flip, z, core),
        device(3 - x, y, z, core),
        device(x, 3 - y, z, core),
    )
    above = device(x, y, (z + 1) % 8, core)
    below = device(x, y, (z + 7) % 8, core)
    sibling = device(x, y, z, 1 - core)

    barrier = pltpu.get_barrier_semaphore()
    for other in (*plane, above, below, sibling):
        pl.semaphore_signal(barrier, inc=1, device_id=other, device_id_type=MESH)

    inputs = [
        pltpu.make_async_copy(src, dst, in_s.at[i])
        for i, (src, dst) in enumerate(((images_in, images), (texts_in, texts)))
    ]
    for c in inputs:
        c.start()
    sent = []

    def copy(src, dst, send, recv, to):
        return pltpu.make_async_remote_copy(
            src_ref=src, dst_ref=dst, send_sem=send, recv_sem=recv, device_id=to, device_id_type=MESH
        )

    def start(c):
        c.start()
        sent.append(c)

    def gather_image(q, s, part):
        a, b = GATHER_PARTS[s][part]
        n = FIRST_PART[s] + part
        return copy(
            img.at[a:b, q], img.at[2**s + a : 2**s + b, q], gi_s.at[q, n], gi_r.at[q, n], plane[(q + s) % 4]
        )

    def gather_text(way, step, half):
        slots = (UP, DOWN)[way]
        src, dst = slots[step], slots[step + 1]
        rows = slice(half * HALF, (half + 1) * HALF)
        return copy(
            txt.at[src, 0, rows], txt.at[dst, 0, rows],
            gt_s.at[way, step, half], gt_r.at[way, step, half], (above, below)[way],
        )

    def share_text(slot, half):
        rows = slice(half * HALF, (half + 1) * HALF)
        return copy(txt.at[slot, 0, rows], txt.at[slot, 1, rows], gc_s.at[slot, half], gc_r.at[slot, half], sibling)

    def reduce_image(q, s, part):
        a, b = REDUCE_PARTS[s][part]
        n = FIRST_PART[s] + part
        return copy(isend.at[a:b, q], irecv.at[a:b, q], ri_s.at[q, n], ri_r.at[q, n], plane[(q + s) % 4])

    def share_sum(slot):
        return copy(csend.at[slot], crecv.at[slot], rc_s.at[slot], rc_r.at[slot], sibling)

    def reduce_text(way, m, half):
        rows = slice(half * HALF, (half + 1) * HALF)
        return copy(
            tsend.at[way, m, rows], trecv.at[way, m, rows],
            rt_s.at[way, m, half], rt_r.at[way, m, half], (above, below)[way],
        )

    def send_stat(n, src, to):
        return copy(stat.at[src], stat.at[n], st_s.at[n], st_r.at[n], to)

    inputs[0].wait()
    img[0] = unit_rows(images)[0].astype(BF16).reshape(4, QUARTER, WIDTH)
    inputs[1].wait()
    txt[0, 0] = unit_rows(texts)[0].astype(BF16)
    scale = jnp.exp(log_scale[...])
    shift = bias[...]
    scale_two = scale * LOG2E
    shift_two = shift * LOG2E
    acc[...] = jnp.zeros_like(acc)
    pl.semaphore_wait(barrier, 7)

    def block(first_row, rows, first_col, columns):
        c = lax.dot_general(
            img[pl.ds(first_row // 64, rows // 64)].reshape(rows, WIDTH),
            txt[first_col // 128 : (first_col + columns) // 128].reshape(columns, WIDTH),
            (((1,), (1,)), ((), ())),
            preferred_element_type=F32,
        )
        e = jnp.exp2(c * scale_two + shift_two)
        gate = e / (1.0 + e)
        w[pl.ds(first_row, rows), first_col : first_col + columns] = (scale * gate).astype(BF16)

        def fold(v):
            v = jnp.sum(v.reshape(-1, 16, columns), axis=0)
            return sum(v[:, k : k + 128] for k in range(0, columns, 128))

        fourth = rows // 4
        a, b = e[: 2 * fourth], e[2 * fourth :]
        a = a + b + a * b
        a, b = a[:fourth], a[fourth:]
        acc[0] = acc[0] + fold(jnp.log1p(a + b + a * b))
        acc[1] = acc[1] + fold(gate * c)
        acc[2] = acc[2] + fold(gate)

    def blocks(first_slot, end_slot, first_text, end_text):
        def one(i, _):
            block(pl.multiple_of(first_slot * 64 + i * 256, 256), 256, first_text * 128, (end_text - first_text) * 128)
            return 0

        lax.fori_loop(0, (end_slot - first_slot) // 4, one, 0)

    def own_pairs():
        c = lax.dot_general(
            img[0].reshape(ROWS, WIDTH),
            txt[0].reshape(2 * ROWS, WIDTH),
            (((1,), (1,)), ((), ())),
            preferred_element_type=F32,
        )
        logit = scale * c + shift
        same = lax.broadcasted_iota(jnp.int32, (ROWS, 128), 0) == lax.broadcasted_iota(jnp.int32, (ROWS, 128), 1)
        match = -scale / (1.0 + jnp.exp(logit))
        w[:ROWS, :128] = jnp.where(same, match, w[:ROWS, :128].astype(F32)).astype(BF16)
        for k, v in enumerate((logit, c, jnp.ones_like(c))):
            acc[k] = acc[k] - jnp.where(same, v, 0.0).reshape(4, 16, 128).sum(axis=0)

    for s in range(4):
        for q in range(4):
            start(gather_image(q, s, 0))
        if s < 2:
            for way in range(2):
                start(gather_text(way, 0, s if way == 0 else 1 - s))
    for half in range(2):
        start(share_text(0, half))

    def pass_text(way, step, half):
        gather_text(way, step, half).wait_recv()
        slot = (UP, DOWN)[way][step + 1]
        if step < 2 or (step == 2 and half == way):
            start(gather_text(way, step + 1, half))
        start(share_text(slot, half))

    def got_image(s, part):
        for q in range(4):
            gather_image(q, s, part).wait_recv()

    def pass_image(stages, part):
        for s in stages:
            for q in range(4):
                start(gather_image(q, s, part))

    def got_shared(slots):
        for slot in slots:
            for half in range(2):
                share_text(slot, half).wait_recv()

    got_image(0, 0)
    pass_image((1, 2, 3), 1)
    for way in range(2):
        pass_text(way, 0, way)
    got_image(1, 0)
    got_image(1, 1)
    pass_image((2, 3), 2)
    for way in range(2):
        pass_text(way, 0, 1 - way)
    got_shared((0, 1, 2))
    blocks(0, 4, 0, 3)
    own_pairs()
    for way in range(2):
        pass_text(way, 1, way)
    for way in range(2):
        pass_text(way, 1, 1 - way)
    for part in range(3):
        got_image(2, part)
    pass_image((3,), 3)
    blocks(4, 8, 0, 3)
    got_shared((3, 4))
    for way in range(2):
        pass_text(way, 2, way)
    blocks(0, 8, 3, 5)
    for way in range(2):
        pass_text(way, 2, 1 - way)
    for part in range(3):
        got_image(3, part)
    blocks(8, 12, 0, 5)
    got_shared((5, 6))
    blocks(0, 4, 5, 7)
    for way in range(2):
        pass_text(way, 3, way)
    blocks(4, 12, 5, 7)
    got_shared((7,))
    got_image(3, 3)
    blocks(12, 16, 0, 8)

    def stat_plane(n):
        return send_stat(n, 0, device((x + n // 4) % 4, (y + n % 4) % 4, z, core))

    def stat_column(n):
        return send_stat(16 + n, 16, device(x, y, (z + n // 2) % 8, (core + n) % 2))

    def stat_own():
        stat[0] = jnp.zeros((8, 128), F32)
        for k in range(3):
            stat[0, k : k + 1] = jnp.sum(acc[k], axis=0, keepdims=True)
        for n in range(1, 16):
            start(stat_plane(n))

    def stat_turn():
        total = stat[0]
        for n in range(1, 16):
            stat_plane(n).wait_recv()
            total = total + stat[n]
        stat[16] = total
        for n in range(1, 16):
            start(stat_column(n))

    def stat_last():
        total = stat[16]
        for n in range(1, 16):
            stat_column(n).wait_recv()
            total = total + stat[16 + n]
        stat_sum[...] = total

    def image_part(slot):
        return jnp.dot(
            w[slot * 64 : (slot + 4) * 64, :], txt[...].reshape(TILE, WIDTH), preferred_element_type=F32
        ).reshape(4, 4, QUARTER, WIDTH)

    def text_part(slot, count):
        part = lax.dot_general(
            w[:, slot * 128 : (slot + count) * 128],
            img[...].reshape(TILE, WIDTH),
            (((0,), (0,)), ((), ())),
            preferred_element_type=F32,
        ).reshape(count, 2, ROWS, WIDTH)
        csend[slot : slot + count] = encode(part[:, 1])
        tacc[slot : slot + count] = part[:, 0]
        for k in range(slot, slot + count):
            start(share_sum(k))

    def send_images(s, parts):
        for part in parts:
            for q in range(4):
                start(reduce_image(q, s, part))

    def wait_images(s, part):
        for q in range(4):
            reduce_image(q, s, part).wait_recv()

    def add_images(first, count, stage, forward):
        def one(i, _):
            slot, q = first + i // 4, i % 4
            total = iacc[slot, q] + decode(irecv[2**stage + slot, q])
            if forward:
                isend[slot, q] = encode(total)
            else:
                iacc[slot, q] = total
            return 0

        lax.fori_loop(0, 4 * count, one, 0)

    def join_texts(slot):
        share_sum(slot).wait_recv()

        def one(i, _):
            rows = pl.ds(pl.multiple_of(i * 16, 16), 16)
            tacc[slot, rows] = tacc[slot, rows] + decode(crecv[slot, rows])
            return 0

        lax.fori_loop(0, 4, one, 0)

    def pass_sum(way, m, half):
        slot = (DOWN, UP)[way][m]
        arrives = m == 3 and half == way or m < 3
        if arrives:
            reduce_text(way, m + 1, half).wait_recv()
        for i in range(2):
            rows = slice(half * HALF + i * 16, half * HALF + (i + 1) * 16)
            total = tacc[slot, rows]
            if arrives:
                total = total + decode(trecv[way, m + 1, rows])
            tsend[way, m, rows] = encode(total)
        start(reduce_text(way, m, half))

    def pass_sums(m, own):
        for way in range(2):
            pass_sum(way, m, way if own else 1 - way)

    isend[12:16] = encode(image_part(12))
    send_images(3, (0,))
    block(0, 768, 896, 128)
    text_part(7, 1)
    stat_own()
    text_part(5, 2)
    join_texts(7)
    pass_sums(4, True)
    isend[8:12] = encode(image_part(8))
    send_images(3, (1, 2, 3))
    join_texts(5)
    join_texts(6)
    pass_sums(3, False)
    text_part(3, 2)
    iacc[4:8] = image_part(4)
    pass_sums(3, True)
    join_texts(3)
    join_texts(4)
    pass_sums(2, False)
    wait_images(3, 0)
    add_images(4, 4, 3, True)
    send_images(2, (0, 1, 2))
    stat_turn()
    iacc[0:4] = image_part(0)
    text_part(0, 3)
    pass_sums(2, True)
    for part in (1, 2, 3):
        wait_images(3, part)
    add_images(0, 4, 3, False)
    for slot in (1, 2, 0):
        join_texts(slot)
    wait_images(2, 0)
    add_images(2, 2, 2, True)
    send_images(1, (0, 1))
    pass_sums(1, False)
    wait_images(2, 1)
    wait_images(2, 2)
    add_images(0, 2, 2, False)
    pass_sums(1, True)
    wait_images(1, 0)
    add_images(1, 1, 1, True)
    send_images(0, (0,))
    wait_images(1, 1)
    add_images(0, 1, 1, False)
    stat_last()

    for way in range(2):
        for half in range(2):
            reduce_text(way, 1, half).wait_recv()
    text_sum[...] = tacc[0] + decode(trecv[0, 1]) + decode(trecv[1, 1])
    wait_images(0, 0)
    image_sum[...] = (iacc[0] + decode(irecv[1])).reshape(ROWS, WIDTH)
    for c in sent:
        c.wait_send()


def finish(images, texts, image_sum, text_sum, stat_sum, log_scale, image_grad, text_grad, loss, scale_grad, bias_grad):
    for raw, total, out in ((images, image_sum, image_grad), (texts, text_sum, text_grad)):
        unit, inverse = unit_rows(raw)
        grad = total[...] * (1.0 / PAIRS)
        out[...] = inverse * (grad - unit * jnp.sum(unit * grad, axis=1, keepdims=True))
    scale = jnp.exp(jnp.broadcast_to(log_scale[...], (1, 128)))
    loss[0] = jnp.sum(stat_sum[0:1]) * (1.0 / PAIRS)
    scale_grad[0] = jnp.sum(stat_sum[1:2] * scale) * (1.0 / PAIRS)
    bias_grad[0] = jnp.sum(stat_sum[2:3]) * (1.0 / PAIRS)


def body(images, texts, log_scale, bias):
    vmem = pl.BlockSpec(memory_space=pltpu.VMEM)
    smem = pl.BlockSpec(memory_space=pltpu.SMEM)
    dma = pltpu.SemaphoreType.DMA
    grad = jax.ShapeDtypeStruct((ROWS, WIDTH), F32)
    scalar = jax.ShapeDtypeStruct((1,), F32)
    log_scale = log_scale.reshape(1, 1)
    image_sum, text_sum, stat_sum = pl.pallas_call(
        kernel,
        out_shape=(grad, grad, jax.ShapeDtypeStruct((8, 128), F32)),
        in_specs=[pl.BlockSpec(memory_space=pl.ANY)] * 2 + [vmem] * 2,
        out_specs=(vmem,) * 3,
        scratch_shapes=[
            pltpu.VMEM((16, 4, QUARTER, WIDTH), BF16),
            pltpu.VMEM((8, 2, ROWS, WIDTH), BF16),
            pltpu.VMEM((TILE, TILE), BF16),
            pltpu.VMEM((8, 4, QUARTER, WIDTH), F32),
            pltpu.VMEM((8, ROWS, WIDTH), F32),
            pltpu.VMEM((16, 4, QUARTER, WIDTH), BF16),
            pltpu.VMEM((16, 4, QUARTER, WIDTH), BF16),
            pltpu.VMEM((8, ROWS, WIDTH), BF16),
            pltpu.VMEM((8, ROWS, WIDTH), BF16),
            pltpu.VMEM((2, 5, ROWS, WIDTH), BF16),
            pltpu.VMEM((2, 5, ROWS, WIDTH), BF16),
            pltpu.VMEM((33, 8, 128), F32),
            pltpu.VMEM((3, 16, 128), F32),
            dma((4, 10)), dma((4, 10)),
            dma((2, 4, 2)), dma((2, 4, 2)),
            dma((8, 2)), dma((8, 2)),
            dma((4, 10)), dma((4, 10)),
            dma((8,)), dma((8,)),
            dma((2, 5, 2)), dma((2, 5, 2)),
            dma((32,)), dma((32,)),
            pltpu.VMEM((ROWS, WIDTH), BF16), pltpu.VMEM((ROWS, WIDTH), BF16), dma((2,)),
        ],
        compiler_params=pltpu.CompilerParams(
            collective_id=0, has_side_effects=True, vmem_limit_bytes=56 * 2**20
        ),
        cost_estimate=pl.CostEstimate(flops=6 * TILE * TILE * WIDTH, bytes_accessed=2**20, transcendentals=2 * TILE * TILE),
        name="pairs",
    )(images, texts, log_scale, bias.reshape(1, 1))
    return pl.pallas_call(
        finish,
        out_shape=(grad, grad, scalar, scalar, scalar),
        in_specs=[vmem] * 6,
        out_specs=(vmem, vmem, smem, smem, smem),
        name="finish",
    )(images, texts, image_sum, text_sum, stat_sum, log_scale)


def solution(mesh):
    rows = P(("row", "col"), None)
    return jax.shard_map(
        body,
        mesh=mesh,
        in_specs=(rows, rows, P(), P()),
        out_specs=(rows, rows, P(), P(), P()),
        check_vma=False,
    )
```

```python
import jax
import jax.numpy as jnp
from jax import lax
from jax.experimental import pallas as pl
from jax.experimental.pallas import tpu as pltpu
from jax.sharding import PartitionSpec as P

MESH = pl.DeviceIdType.MESH
F32 = jnp.float32
BF16 = jnp.bfloat16
ROWS = 64
QUARTER = 16
HALF = 32
WIDTH = 1152
PAIRS = 16384
LOG2E = 1.4426950408889634
TILE = 1024

GATHER_PARTS = (
    ((0, 1),),
    ((0, 1), (1, 2)),
    ((0, 1), (1, 2), (2, 4)),
    ((0, 1), (1, 2), (2, 4), (4, 6), (6, 8)),
)
REDUCE_PARTS = (
    ((1, 2),),
    ((3, 4), (2, 3)),
    ((6, 8), (5, 6), (4, 5)),
    ((12, 16), (10, 12), (9, 10), (8, 9)),
)
FIRST_PART = (0, 1, 3, 6)
UP = {0: 0, 1: 2, 2: 4, 3: 6, 4: 7}
DOWN = {0: 0, 1: 1, 2: 3, 3: 5, 4: 7}


def unit_rows(raw):
    values = raw[...].astype(F32)
    inverse = lax.rsqrt(jnp.sum(values * values, axis=1, keepdims=True) + 1e-06)
    return values * inverse, inverse


def encode(v):
    squared = v * v
    return (v * jnp.abs(v) * squared).astype(BF16)


def decode(y):
    y = y.astype(F32)
    inverse = lax.rsqrt(jnp.maximum(jnp.abs(y), 1e-37))
    return y * inverse * inverse * lax.rsqrt(inverse)


def kernel(
    images_in, texts_in, log_scale, bias,
    image_sum, text_sum, stat_sum,
    img, txt, w, iacc, tacc, isend, irecv, csend, crecv, tsend, trecv, stat, acc,
    gi_s, gi_r, gt_s, gt_r, gc_s, gc_r, ri_s, ri_r, rc_s, rc_r, rt_s, rt_r, st_s, st_r, images, texts, in_s,
):
    row = lax.axis_index("row")
    col = lax.axis_index("col")
    x = 2 * (col // 4) + (row // 2) % 2
    y = col % 4
    z = row // 4
    core = row % 2

    def device(x, y, z, core):
        return (z * 4 + (x % 2) * 2 + core, (x // 2) * 4 + y)

    x_flip = x + 1 - 2 * (x % 2)
    y_flip = y + 1 - 2 * (y % 2)
    plane = (
        device(x_flip, y, z, core),
        device(x, y_flip, z, core),
        device(3 - x, y, z, core),
        device(x, 3 - y, z, core),
    )
    above = device(x, y, (z + 1) % 8, core)
    below = device(x, y, (z + 7) % 8, core)
    sibling = device(x, y, z, 1 - core)

    barrier = pltpu.get_barrier_semaphore()
    for other in (*plane, above, below, sibling):
        pl.semaphore_signal(barrier, inc=1, device_id=other, device_id_type=MESH)

    inputs = [
        pltpu.make_async_copy(src, dst, in_s.at[i])
        for i, (src, dst) in enumerate(((images_in, images), (texts_in, texts)))
    ]
    for c in inputs:
        c.start()

    def copy(src, dst, send, recv, to):
        return pltpu.make_async_remote_copy(
            src_ref=src, dst_ref=dst, send_sem=send, recv_sem=recv, device_id=to, device_id_type=MESH
        )

    def start(c):
        c.start()

    def gather_image(q, s, part):
        a, b = GATHER_PARTS[s][part]
        n = FIRST_PART[s] + part
        return copy(
            img.at[a:b, q], img.at[2**s + a : 2**s + b, q], gi_s, gi_r.at[n], plane[(q + s) % 4]
        )

    def gather_text(way, step, half):
        slots = (UP, DOWN)[way]
        src, dst = slots[step], slots[step + 1]
        rows = slice(half * HALF, (half + 1) * HALF)
        return copy(
            txt.at[src, 0, rows], txt.at[dst, 0, rows],
            gt_s, gt_r.at[way, step, half], (above, below)[way],
        )

    def share_text(slot, half):
        rows = slice(half * HALF, (half + 1) * HALF)
        return copy(txt.at[slot, 0, rows], txt.at[slot, 1, rows], gc_s, gc_r.at[slot, half], sibling)

    def reduce_image(q, s, part):
        a, b = REDUCE_PARTS[s][part]
        n = FIRST_PART[s] + part
        return copy(isend.at[a:b, q], irecv.at[a:b, q], ri_s, ri_r.at[n], plane[(q + s) % 4])

    def share_sum(slot):
        return copy(csend.at[slot], crecv.at[slot], rc_s, rc_r.at[slot], sibling)

    def reduce_text(way, m, half):
        rows = slice(half * HALF, (half + 1) * HALF)
        return copy(
            tsend.at[way, m, rows], trecv.at[way, m, rows],
            rt_s, rt_r.at[way, m, half], (above, below)[way],
        )

    def send_stat(n, src, to):
        return copy(stat.at[src], stat.at[n], st_s, st_r.at[n // 16], to)

    inputs[0].wait()
    img[0] = unit_rows(images)[0].astype(BF16).reshape(4, QUARTER, WIDTH)
    inputs[1].wait()
    txt[0, 0] = unit_rows(texts)[0].astype(BF16)
    scale = jnp.exp(log_scale[...])
    shift = bias[...]
    scale_two = scale * LOG2E
    shift_two = shift * LOG2E
    acc[...] = jnp.zeros_like(acc)
    pl.semaphore_wait(barrier, 7)

    def block(first_row, rows, first_col, columns):
        c = lax.dot_general(
            img[pl.ds(first_row // 64, rows // 64)].reshape(rows, WIDTH),
            txt[first_col // 128 : (first_col + columns) // 128].reshape(columns, WIDTH),
            (((1,), (1,)), ((), ())),
            preferred_element_type=F32,
        )
        e = jnp.exp2(c * scale_two + shift_two)
        gate = e / (1.0 + e)
        w[pl.ds(first_row, rows), first_col : first_col + columns] = (scale * gate).astype(BF16)

        def fold(v):
            v = jnp.sum(v.reshape(-1, 16, columns), axis=0)
            return sum(v[:, k : k + 128] for k in range(0, columns, 128))

        fourth = rows // 4
        a, b = e[: 2 * fourth], e[2 * fourth :]
        a = a + b + a * b
        a, b = a[:fourth], a[fourth:]
        acc[0] = acc[0] + fold(jnp.log1p(a + b + a * b))
        acc[1] = acc[1] + fold(gate * c)
        acc[2] = acc[2] + fold(gate)

    def blocks(first_slot, end_slot, first_text, end_text):
        def one(i, _):
            block(pl.multiple_of(first_slot * 64 + i * 256, 256), 256, first_text * 128, (end_text - first_text) * 128)
            return 0

        lax.fori_loop(0, (end_slot - first_slot) // 4, one, 0)

    def own_pairs():
        c = lax.dot_general(
            img[0].reshape(ROWS, WIDTH),
            txt[0].reshape(2 * ROWS, WIDTH),
            (((1,), (1,)), ((), ())),
            preferred_element_type=F32,
        )
        logit = scale * c + shift
        same = lax.broadcasted_iota(jnp.int32, (ROWS, 128), 0) == lax.broadcasted_iota(jnp.int32, (ROWS, 128), 1)
        match = -scale / (1.0 + jnp.exp(logit))
        w[:ROWS, :128] = jnp.where(same, match, w[:ROWS, :128].astype(F32)).astype(BF16)
        for k, v in enumerate((logit, c, jnp.ones_like(c))):
            acc[k] = acc[k] - jnp.where(same, v, 0.0).reshape(4, 16, 128).sum(axis=0)

    for s in range(4):
        for q in range(4):
            start(gather_image(q, s, 0))
        if s < 2:
            for way in range(2):
                start(gather_text(way, 0, s if way == 0 else 1 - s))
    for half in range(2):
        start(share_text(0, half))

    def pass_text(way, step, half):
        gather_text(way, step, half).wait_recv()
        slot = (UP, DOWN)[way][step + 1]
        if step < 2 or (step == 2 and half == way):
            start(gather_text(way, step + 1, half))
        start(share_text(slot, half))

    def got_image(s, part):
        a, b = GATHER_PARTS[s][part]
        all_four = img.at[2**s + a : 2**s + b]
        copy(all_four, all_four, gi_s, gi_r.at[FIRST_PART[s] + part], sibling).wait_recv()

    def pass_image(stages, part):
        for s in stages:
            for q in range(4):
                start(gather_image(q, s, part))

    def got_shared(slots):
        for slot in slots:
            for half in range(2):
                share_text(slot, half).wait_recv()

    got_image(0, 0)
    pass_image((1, 2, 3), 1)
    for way in range(2):
        pass_text(way, 0, way)
    for way in range(2):
        pass_text(way, 0, 1 - way)
    got_image(1, 0)
    got_image(1, 1)
    pass_image((2, 3), 2)
    got_shared((0, 1, 2))
    blocks(0, 4, 0, 3)
    own_pairs()
    for way in range(2):
        pass_text(way, 1, way)
    for way in range(2):
        pass_text(way, 1, 1 - way)
    for part in range(3):
        got_image(2, part)
    pass_image((3,), 3)
    pass_image((3,), 4)
    blocks(4, 8, 0, 3)
    got_shared((3, 4))
    for way in range(2):
        pass_text(way, 2, way)
    blocks(0, 8, 3, 5)
    for part in range(3):
        got_image(3, part)
    for way in range(2):
        pass_text(way, 2, 1 - way)
    blocks(8, 12, 0, 5)
    got_shared((5, 6))
    blocks(0, 4, 5, 7)
    for way in range(2):
        pass_text(way, 3, way)
    blocks(4, 12, 5, 7)
    got_image(3, 3)
    block(12 * ROWS, 128, 0, 896)
    got_image(3, 4)
    block(14 * ROWS, 128, 0, 896)
    got_shared((7,))
    block(0, TILE, 896, 128)

    def stat_plane(n):
        return send_stat(n, 0, device((x + n // 4) % 4, (y + n % 4) % 4, z, core))

    def stat_column(n):
        return send_stat(16 + n, 16, device(x, y, (z + n // 2) % 8, (core + n) % 2))

    def stat_own():
        stat[0] = jnp.zeros((8, 128), F32)
        for k in range(3):
            stat[0, k : k + 1] = jnp.sum(acc[k], axis=0, keepdims=True)
        for n in range(1, 16):
            start(stat_plane(n))

    def stat_turn():
        copy(stat.at[1:16], stat.at[1:16], st_s, st_r.at[0], sibling).wait_recv()
        total = stat[0]
        for n in range(1, 16):
            total = total + stat[n]
        stat[16] = total
        for n in range(1, 16):
            start(stat_column(n))

    def stat_last():
        copy(stat.at[17:32], stat.at[17:32], st_s, st_r.at[1], sibling).wait_recv()
        total = stat[16]
        for n in range(17, 32):
            total = total + stat[n]
        stat_sum[...] = total

    def image_part(slot):
        return jnp.dot(
            w[slot * 64 : (slot + 4) * 64, :], txt[...].reshape(TILE, WIDTH), preferred_element_type=F32
        ).reshape(4, 4, QUARTER, WIDTH)

    def text_part(slot, count):
        part = lax.dot_general(
            w[:, slot * 128 : (slot + count) * 128],
            img[...].reshape(TILE, WIDTH),
            (((0,), (0,)), ((), ())),
            preferred_element_type=F32,
        ).reshape(count, 2, ROWS, WIDTH)
        csend[slot : slot + count] = encode(part[:, 1])
        tacc[slot : slot + count] = part[:, 0]
        for k in range(slot, slot + count):
            start(share_sum(k))

    def send_images(s, parts):
        for part in parts:
            for q in range(4):
                start(reduce_image(q, s, part))

    def wait_images(s, part):
        a, b = REDUCE_PARTS[s][part]
        copy(isend.at[a:b], irecv.at[a:b], ri_s, ri_r.at[FIRST_PART[s] + part], sibling).wait_recv()

    def add_images(first, count, stage, forward):
        def one(i, _):
            slot = first + i
            total = iacc[slot] + decode(irecv[2**stage + slot])
            if forward:
                isend[slot] = encode(total)
            else:
                iacc[slot] = total
            return 0

        lax.fori_loop(0, count, one, 0)

    def join_texts(slot):
        share_sum(slot).wait_recv()
        tacc[slot] = tacc[slot] + decode(crecv[slot])

    def pass_sum(way, m, half):
        slot = (DOWN, UP)[way][m]
        arrives = m == 3 and half == way or m < 3
        if arrives:
            reduce_text(way, m + 1, half).wait_recv()
        rows = slice(half * HALF, (half + 1) * HALF)
        total = tacc[slot, rows]
        if arrives:
            total = total + decode(trecv[way, m + 1, rows])
        tsend[way, m, rows] = encode(total)
        start(reduce_text(way, m, half))

    def pass_sums(m, own):
        for way in range(2):
            pass_sum(way, m, way if own else 1 - way)

    isend[12:16] = encode(image_part(12))
    send_images(3, (0,))
    text_part(7, 1)
    text_part(5, 2)
    join_texts(7)
    pass_sums(4, True)
    stat_own()
    isend[8:12] = encode(image_part(8))
    send_images(3, (1, 2, 3))
    join_texts(5)
    join_texts(6)
    pass_sums(3, False)
    text_part(3, 2)
    iacc[4:8] = image_part(4)
    pass_sums(3, True)
    wait_images(3, 0)
    add_images(4, 4, 3, True)
    send_images(2, (0, 1, 2))
    join_texts(3)
    join_texts(4)
    pass_sums(2, False)
    stat_turn()
    iacc[0:4] = image_part(0)
    text_part(0, 3)
    pass_sums(2, True)
    for part in (1, 2, 3):
        wait_images(3, part)
    add_images(0, 4, 3, False)
    for slot in (1, 2, 0):
        join_texts(slot)
    wait_images(2, 0)
    add_images(2, 2, 2, True)
    send_images(1, (0, 1))
    pass_sums(1, False)
    wait_images(2, 1)
    wait_images(2, 2)
    add_images(0, 2, 2, False)
    pass_sums(1, True)
    wait_images(1, 0)
    add_images(1, 1, 1, True)
    send_images(0, (0,))
    wait_images(1, 1)
    add_images(0, 1, 1, False)
    stat_last()

    for way in range(2):
        for half in range(2):
            reduce_text(way, 1, half).wait_recv()
    text_sum[...] = tacc[0] + decode(trecv[0, 1]) + decode(trecv[1, 1])
    wait_images(0, 0)
    image_sum[...] = (iacc[0] + decode(irecv[1])).reshape(ROWS, WIDTH)
    for view, sem in (
        (img.at[0:15], gi_s),
        (txt.at[0:7, 0], gt_s),
        (txt.at[0:8, 0], gc_s),
        (isend.at[1:16], ri_s),
        (csend.at[0:8], rc_s),
        (csend.at[0:7], rt_s),
        (stat.at[0:30], st_s),
    ):
        copy(view, view, sem, in_s.at[0], sibling).wait_send()


def finish(images, texts, image_sum, text_sum, stat_sum, log_scale, image_grad, text_grad, loss, scale_grad, bias_grad):
    for raw, total, out in ((images, image_sum, image_grad), (texts, text_sum, text_grad)):
        unit, inverse = unit_rows(raw)
        grad = total[...] * (1.0 / PAIRS)
        out[...] = inverse * (grad - unit * jnp.sum(unit * grad, axis=1, keepdims=True))
    scale = jnp.exp(jnp.broadcast_to(log_scale[...], (1, 128)))
    loss[0] = jnp.sum(stat_sum[0:1]) * (1.0 / PAIRS)
    scale_grad[0] = jnp.sum(stat_sum[1:2] * scale) * (1.0 / PAIRS)
    bias_grad[0] = jnp.sum(stat_sum[2:3]) * (1.0 / PAIRS)


def body(images, texts, log_scale, bias):
    vmem = pl.BlockSpec(memory_space=pltpu.VMEM)
    smem = pl.BlockSpec(memory_space=pltpu.SMEM)
    dma = pltpu.SemaphoreType.DMA
    grad = jax.ShapeDtypeStruct((ROWS, WIDTH), F32)
    scalar = jax.ShapeDtypeStruct((1,), F32)
    log_scale = log_scale.reshape(1, 1)
    image_sum, text_sum, stat_sum = pl.pallas_call(
        kernel,
        out_shape=(grad, grad, jax.ShapeDtypeStruct((8, 128), F32)),
        in_specs=[pl.BlockSpec(memory_space=pl.ANY)] * 2 + [vmem] * 2,
        out_specs=(vmem,) * 3,
        scratch_shapes=[
            pltpu.VMEM((16, 4, QUARTER, WIDTH), BF16),
            pltpu.VMEM((8, 2, ROWS, WIDTH), BF16),
            pltpu.VMEM((TILE, TILE), BF16),
            pltpu.VMEM((8, 4, QUARTER, WIDTH), F32),
            pltpu.VMEM((8, ROWS, WIDTH), F32),
            pltpu.VMEM((16, 4, QUARTER, WIDTH), BF16),
            pltpu.VMEM((16, 4, QUARTER, WIDTH), BF16),
            pltpu.VMEM((8, ROWS, WIDTH), BF16),
            pltpu.VMEM((8, ROWS, WIDTH), BF16),
            pltpu.VMEM((2, 5, ROWS, WIDTH), BF16),
            pltpu.VMEM((2, 5, ROWS, WIDTH), BF16),
            pltpu.VMEM((33, 8, 128), F32),
            pltpu.VMEM((3, 16, 128), F32),
            dma(()), dma((11,)),
            dma(()), dma((2, 4, 2)),
            dma(()), dma((8, 2)),
            dma(()), dma((10,)),
            dma(()), dma((8,)),
            dma(()), dma((2, 5, 2)),
            dma(()), dma((2,)),
            pltpu.VMEM((ROWS, WIDTH), BF16), pltpu.VMEM((ROWS, WIDTH), BF16), dma((2,)),
        ],
        compiler_params=pltpu.CompilerParams(
            collective_id=0, has_side_effects=True, vmem_limit_bytes=56 * 2**20
        ),
        cost_estimate=pl.CostEstimate(flops=6 * TILE * TILE * WIDTH, bytes_accessed=2**20, transcendentals=2 * TILE * TILE),
        name="pairs",
    )(images, texts, log_scale, bias.reshape(1, 1))
    return pl.pallas_call(
        finish,
        out_shape=(grad, grad, scalar, scalar, scalar),
        in_specs=[vmem] * 6,
        out_specs=(vmem, vmem, smem, smem, smem),
        name="finish",
    )(images, texts, image_sum, text_sum, stat_sum, log_scale)


def solution(mesh):
    rows = P(("row", "col"), None)
    return jax.shard_map(
        body,
        mesh=mesh,
        in_specs=(rows, rows, P(), P()),
        out_specs=(rows, rows, P(), P(), P()),
        check_vma=False,
    )
```

```python
import jax
import jax.numpy as jnp
from jax import lax
from jax.experimental import pallas as pl
from jax.experimental.pallas import tpu as pltpu
from jax.sharding import PartitionSpec as P

MESH = pl.DeviceIdType.MESH
F32 = jnp.float32
BF16 = jnp.bfloat16
ROWS = 64
QUARTER = 16
HALF = 32
WIDTH = 1152
PAIRS = 16384
LOG2E = 1.4426950408889634
TILE = 1024

GATHER_PARTS = (
    ((0, 1),),
    ((0, 1), (1, 2)),
    ((0, 1), (1, 2), (2, 4)),
    ((0, 1), (1, 2), (2, 4), (4, 6), (6, 8)),
)
REDUCE_PARTS = (
    ((1, 2),),
    ((3, 4), (2, 3)),
    ((6, 8), (5, 6), (4, 5)),
    ((12, 16), (10, 12), (9, 10), (8, 9)),
)
FIRST_PART = (0, 1, 3, 6)
UP = {0: 0, 1: 2, 2: 4, 3: 6, 4: 7}
DOWN = {0: 0, 1: 1, 2: 3, 3: 5, 4: 7}


def unit_rows(raw):
    values = raw[...].astype(F32)
    inverse = lax.rsqrt(jnp.sum(values * values, axis=1, keepdims=True) + 1e-06)
    return values * inverse, inverse


def encode(v):
    squared = v * v
    return (v * jnp.abs(v) * squared).astype(BF16)


def decode(y):
    y = y.astype(F32)
    inverse = lax.rsqrt(jnp.maximum(jnp.abs(y), 1e-37))
    return y * inverse * inverse * lax.rsqrt(inverse)


def kernel(
    images_in, texts_in, log_scale, bias,
    image_sum, text_sum, stat_sum,
    img, txt, w, iacc, tacc, isend, irecv, csend, crecv, tsend, trecv, stat, acc,
    gi_s, gi_r, gt_s, gt_r, gc_s, gc_r, ri_s, ri_r, rc_s, rc_r, rt_s, rt_r, st_s, st_r, images, texts, in_s,
):
    row = lax.axis_index("row")
    col = lax.axis_index("col")
    x = 2 * (col // 4) + (row // 2) % 2
    y = col % 4
    z = row // 4
    core = row % 2

    def device(x, y, z, core):
        return (z * 4 + (x % 2) * 2 + core, (x // 2) * 4 + y)

    x_flip = x + 1 - 2 * (x % 2)
    y_flip = y + 1 - 2 * (y % 2)
    plane = (
        device(x_flip, y, z, core),
        device(x, y_flip, z, core),
        device(3 - x, y, z, core),
        device(x, 3 - y, z, core),
    )
    above = device(x, y, (z + 1) % 8, core)
    below = device(x, y, (z + 7) % 8, core)
    sibling = device(x, y, z, 1 - core)

    barrier = pltpu.get_barrier_semaphore()
    for other in (*plane, above, below, sibling):
        pl.semaphore_signal(barrier, inc=1, device_id=other, device_id_type=MESH)

    inputs = [
        pltpu.make_async_copy(src, dst, in_s.at[i])
        for i, (src, dst) in enumerate(((images_in, images), (texts_in, texts)))
    ]
    for c in inputs:
        c.start()

    def copy(src, dst, send, recv, to):
        return pltpu.make_async_remote_copy(
            src_ref=src, dst_ref=dst, send_sem=send, recv_sem=recv, device_id=to, device_id_type=MESH
        )

    def start(c):
        c.start()

    def gather_image(q, s, part):
        a, b = GATHER_PARTS[s][part]
        n = FIRST_PART[s] + part
        return copy(
            img.at[a:b, q], img.at[2**s + a : 2**s + b, q], gi_s, gi_r.at[n], plane[(q + s) % 4]
        )

    def gather_text(way, step, half):
        slots = (UP, DOWN)[way]
        src, dst = slots[step], slots[step + 1]
        rows = slice(half * HALF, (half + 1) * HALF)
        return copy(
            txt.at[src, 0, rows], txt.at[dst, 0, rows],
            gt_s, gt_r.at[way, step, half], (above, below)[way],
        )

    def share_text(slot, half):
        rows = slice(half * HALF, (half + 1) * HALF)
        return copy(txt.at[slot, 0, rows], txt.at[slot, 1, rows], gc_s, gc_r.at[slot, half], sibling)

    def reduce_image(q, s, part):
        a, b = REDUCE_PARTS[s][part]
        n = FIRST_PART[s] + part
        return copy(isend.at[a:b, q], irecv.at[a:b, q], ri_s, ri_r.at[n], plane[(q + s) % 4])

    def share_sum(slot):
        return copy(csend.at[slot], crecv.at[slot], rc_s, rc_r.at[slot], sibling)

    def reduce_text(way, m, half):
        rows = slice(half * HALF, (half + 1) * HALF)
        return copy(
            tsend.at[way, m, rows], trecv.at[way, m, rows],
            rt_s, rt_r.at[way, m, half], (above, below)[way],
        )

    def send_stat(n, src, to):
        return copy(stat.at[src], stat.at[n], st_s, st_r.at[n // 16], to)

    inputs[0].wait()
    img[0] = unit_rows(images)[0].astype(BF16).reshape(4, QUARTER, WIDTH)
    inputs[1].wait()
    txt[0, 0] = unit_rows(texts)[0].astype(BF16)
    scale = jnp.exp(log_scale[...])
    shift = bias[...]
    scale_two = scale * LOG2E
    shift_two = shift * LOG2E
    acc[...] = jnp.zeros_like(acc)
    pl.semaphore_wait(barrier, 7)

    def block(first_row, rows, first_col, columns):
        c = lax.dot_general(
            img[pl.ds(first_row // 64, rows // 64)].reshape(rows, WIDTH),
            txt[first_col // 128 : (first_col + columns) // 128].reshape(columns, WIDTH),
            (((1,), (1,)), ((), ())),
            preferred_element_type=F32,
        )
        e = jnp.exp2(c * scale_two + shift_two)
        gate = e / (1.0 + e)
        w[pl.ds(first_row, rows), first_col : first_col + columns] = (scale * gate).astype(BF16)

        def fold(v):
            v = jnp.sum(v.reshape(-1, 16, columns), axis=0)
            return sum(v[:, k : k + 128] for k in range(0, columns, 128))

        fourth = rows // 4
        a, b = e[: 2 * fourth], e[2 * fourth :]
        a = a + b + a * b
        a, b = a[:fourth], a[fourth:]
        acc[0] = acc[0] + fold(jnp.log1p(a + b + a * b))
        acc[1] = acc[1] + fold(gate * c)
        acc[2] = acc[2] + fold(gate)

    def blocks(first_slot, end_slot, first_text, end_text):
        def one(i, _):
            block(pl.multiple_of(first_slot * 64 + i * 256, 256), 256, first_text * 128, (end_text - first_text) * 128)
            return 0

        lax.fori_loop(0, (end_slot - first_slot) // 4, one, 0)

    def own_pairs():
        c = lax.dot_general(
            img[0].reshape(ROWS, WIDTH),
            txt[0].reshape(2 * ROWS, WIDTH),
            (((1,), (1,)), ((), ())),
            preferred_element_type=F32,
        )
        logit = scale * c + shift
        same = lax.broadcasted_iota(jnp.int32, (ROWS, 128), 0) == lax.broadcasted_iota(jnp.int32, (ROWS, 128), 1)
        match = -scale / (1.0 + jnp.exp(logit))
        w[:ROWS, :128] = jnp.where(same, match, w[:ROWS, :128].astype(F32)).astype(BF16)
        for k, v in enumerate((logit, c, jnp.ones_like(c))):
            acc[k] = acc[k] - jnp.where(same, v, 0.0).reshape(4, 16, 128).sum(axis=0)

    for s in range(4):
        for q in range(4):
            start(gather_image(q, s, 0))
        if s < 2:
            for way in range(2):
                start(gather_text(way, 0, s if way == 0 else 1 - s))
    for half in range(2):
        start(share_text(0, half))

    def pass_text(way, step, half):
        gather_text(way, step, half).wait_recv()
        slot = (UP, DOWN)[way][step + 1]
        if step < 2 or (step == 2 and half == way):
            start(gather_text(way, step + 1, half))
        start(share_text(slot, half))

    def got_image(s, part):
        a, b = GATHER_PARTS[s][part]
        all_four = img.at[2**s + a : 2**s + b]
        copy(all_four, all_four, gi_s, gi_r.at[FIRST_PART[s] + part], sibling).wait_recv()

    def pass_image(stages, part):
        for s in stages:
            for q in range(4):
                start(gather_image(q, s, part))

    def got_shared(slots):
        for slot in slots:
            for half in range(2):
                share_text(slot, half).wait_recv()

    got_image(0, 0)
    pass_image((1, 2, 3), 1)
    for way in range(2):
        pass_text(way, 0, way)
    for way in range(2):
        pass_text(way, 0, 1 - way)
    got_image(1, 0)
    got_image(1, 1)
    pass_image((2, 3), 2)
    got_shared((0, 1, 2))
    blocks(0, 4, 0, 3)
    own_pairs()
    for way in range(2):
        pass_text(way, 1, way)
    for way in range(2):
        pass_text(way, 1, 1 - way)
    for part in range(3):
        got_image(2, part)
    pass_image((3,), 3)
    pass_image((3,), 4)
    blocks(4, 8, 0, 3)
    got_shared((3, 4))
    for way in range(2):
        pass_text(way, 2, way)
    blocks(0, 8, 3, 5)
    for part in range(3):
        got_image(3, part)
    for way in range(2):
        pass_text(way, 2, 1 - way)
    blocks(8, 12, 0, 5)
    got_shared((5, 6))
    blocks(0, 4, 5, 7)
    for way in range(2):
        pass_text(way, 3, way)
    blocks(4, 12, 5, 7)
    got_image(3, 3)
    block(12 * ROWS, 128, 0, 896)
    got_image(3, 4)
    block(14 * ROWS, 128, 0, 896)
    got_shared((7,))
    block(0, TILE, 896, 128)

    def stat_plane(n):
        return send_stat(n, 0, device((x + n // 4) % 4, (y + n % 4) % 4, z, core))

    def stat_column(n):
        return send_stat(16 + n, 16, device(x, y, (z + n // 2) % 8, (core + n) % 2))

    def stat_own():
        stat[0] = jnp.zeros((8, 128), F32)
        for k in range(3):
            stat[0, k : k + 1] = jnp.sum(acc[k], axis=0, keepdims=True)
        for n in range(1, 16):
            start(stat_plane(n))

    def stat_turn():
        copy(stat.at[1:16], stat.at[1:16], st_s, st_r.at[0], sibling).wait_recv()
        total = stat[0]
        for n in range(1, 16):
            total = total + stat[n]
        stat[16] = total
        for n in range(1, 16):
            start(stat_column(n))

    def stat_last():
        copy(stat.at[17:32], stat.at[17:32], st_s, st_r.at[1], sibling).wait_recv()
        total = stat[16]
        for n in range(17, 32):
            total = total + stat[n]
        stat_sum[...] = total

    def image_part(slot):
        return jnp.dot(
            w[slot * 64 : (slot + 4) * 64, :], txt[...].reshape(TILE, WIDTH), preferred_element_type=F32
        ).reshape(4, 4, QUARTER, WIDTH)

    def text_part(slot, count):
        part = lax.dot_general(
            w[:, slot * 128 : (slot + count) * 128],
            img[...].reshape(TILE, WIDTH),
            (((0,), (0,)), ((), ())),
            preferred_element_type=F32,
        ).reshape(count, 2, ROWS, WIDTH)
        csend[slot : slot + count] = encode(part[:, 1])
        tacc[slot : slot + count] = part[:, 0]
        for k in range(slot, slot + count):
            start(share_sum(k))

    def send_images(s, parts):
        for part in parts:
            for q in range(4):
                start(reduce_image(q, s, part))

    def wait_images(s, part):
        a, b = REDUCE_PARTS[s][part]
        copy(isend.at[a:b], irecv.at[a:b], ri_s, ri_r.at[FIRST_PART[s] + part], sibling).wait_recv()

    def add_images(first, count, stage, forward):
        def one(i, _):
            slot = first + i
            total = iacc[slot] + decode(irecv[2**stage + slot])
            if forward:
                isend[slot] = encode(total)
            else:
                iacc[slot] = total
            return 0

        lax.fori_loop(0, count, one, 0)

    def join_texts(slot):
        share_sum(slot).wait_recv()
        tacc[slot] = tacc[slot] + decode(crecv[slot])

    def pass_sum(way, m, half):
        slot = (DOWN, UP)[way][m]
        arrives = m == 3 and half == way or m < 3
        if arrives:
            reduce_text(way, m + 1, half).wait_recv()
        rows = slice(half * HALF, (half + 1) * HALF)
        total = tacc[slot, rows]
        if arrives:
            total = total + decode(trecv[way, m + 1, rows])
        tsend[way, m, rows] = encode(total)
        start(reduce_text(way, m, half))

    def pass_sums(m, own):
        for way in range(2):
            pass_sum(way, m, way if own else 1 - way)

    isend[12:16] = encode(image_part(12))
    send_images(3, (0,))
    text_part(7, 1)
    text_part(5, 2)
    join_texts(7)
    pass_sums(4, True)
    stat_own()
    isend[8:12] = encode(image_part(8))
    send_images(3, (1, 2, 3))
    join_texts(5)
    join_texts(6)
    pass_sums(3, False)
    text_part(3, 2)
    pass_sums(3, True)
    wait_images(3, 0)
    isend[4:8] = encode(image_part(4) + decode(irecv[12:16]))
    send_images(2, (0, 1, 2))
    join_texts(3)
    join_texts(4)
    pass_sums(2, False)
    stat_turn()
    iacc[0:4] = image_part(0)
    text_part(0, 3)
    pass_sums(2, True)
    for part in (1, 2, 3):
        wait_images(3, part)
    add_images(2, 2, 3, False)
    wait_images(2, 0)
    add_images(3, 1, 2, True)
    send_images(1, (0,))
    add_images(2, 1, 2, True)
    send_images(1, (1,))
    join_texts(1)
    join_texts(2)
    pass_sums(1, False)
    add_images(0, 2, 3, False)
    join_texts(0)
    wait_images(2, 1)
    wait_images(2, 2)
    add_images(0, 2, 2, False)
    pass_sums(1, True)
    wait_images(1, 0)
    add_images(1, 1, 1, True)
    send_images(0, (0,))
    wait_images(1, 1)
    add_images(0, 1, 1, False)
    stat_last()

    for way in range(2):
        for half in range(2):
            reduce_text(way, 1, half).wait_recv()
    text_sum[...] = tacc[0] + decode(trecv[0, 1]) + decode(trecv[1, 1])
    wait_images(0, 0)
    image_sum[...] = (iacc[0] + decode(irecv[1])).reshape(ROWS, WIDTH)
    for view, sem in (
        (img.at[0:15], gi_s),
        (txt.at[0:7, 0], gt_s),
        (txt.at[0:8, 0], gc_s),
        (isend.at[1:16], ri_s),
        (csend.at[0:8], rc_s),
        (csend.at[0:7], rt_s),
        (stat.at[0:30], st_s),
    ):
        copy(view, view, sem, in_s.at[0], sibling).wait_send()


def finish(images, texts, image_sum, text_sum, stat_sum, log_scale, image_grad, text_grad, loss, scale_grad, bias_grad):
    for raw, total, out in ((images, image_sum, image_grad), (texts, text_sum, text_grad)):
        unit, inverse = unit_rows(raw)
        grad = total[...] * (1.0 / PAIRS)
        out[...] = inverse * (grad - unit * jnp.sum(unit * grad, axis=1, keepdims=True))
    scale = jnp.exp(jnp.broadcast_to(log_scale[...], (1, 128)))
    loss[0] = jnp.sum(stat_sum[0:1]) * (1.0 / PAIRS)
    scale_grad[0] = jnp.sum(stat_sum[1:2] * scale) * (1.0 / PAIRS)
    bias_grad[0] = jnp.sum(stat_sum[2:3]) * (1.0 / PAIRS)


def body(images, texts, log_scale, bias):
    vmem = pl.BlockSpec(memory_space=pltpu.VMEM)
    smem = pl.BlockSpec(memory_space=pltpu.SMEM)
    dma = pltpu.SemaphoreType.DMA
    grad = jax.ShapeDtypeStruct((ROWS, WIDTH), F32)
    scalar = jax.ShapeDtypeStruct((1,), F32)
    log_scale = log_scale.reshape(1, 1)
    image_sum, text_sum, stat_sum = pl.pallas_call(
        kernel,
        out_shape=(grad, grad, jax.ShapeDtypeStruct((8, 128), F32)),
        in_specs=[pl.BlockSpec(memory_space=pl.ANY)] * 2 + [vmem] * 2,
        out_specs=(vmem,) * 3,
        scratch_shapes=[
            pltpu.VMEM((16, 4, QUARTER, WIDTH), BF16),
            pltpu.VMEM((8, 2, ROWS, WIDTH), BF16),
            pltpu.VMEM((TILE, TILE), BF16),
            pltpu.VMEM((8, 4, QUARTER, WIDTH), F32),
            pltpu.VMEM((8, ROWS, WIDTH), F32),
            pltpu.VMEM((16, 4, QUARTER, WIDTH), BF16),
            pltpu.VMEM((16, 4, QUARTER, WIDTH), BF16),
            pltpu.VMEM((8, ROWS, WIDTH), BF16),
            pltpu.VMEM((8, ROWS, WIDTH), BF16),
            pltpu.VMEM((2, 5, ROWS, WIDTH), BF16),
            pltpu.VMEM((2, 5, ROWS, WIDTH), BF16),
            pltpu.VMEM((33, 8, 128), F32),
            pltpu.VMEM((3, 16, 128), F32),
            dma(()), dma((11,)),
            dma(()), dma((2, 4, 2)),
            dma(()), dma((8, 2)),
            dma(()), dma((10,)),
            dma(()), dma((8,)),
            dma(()), dma((2, 5, 2)),
            dma(()), dma((2,)),
            pltpu.VMEM((ROWS, WIDTH), BF16), pltpu.VMEM((ROWS, WIDTH), BF16), dma((2,)),
        ],
        compiler_params=pltpu.CompilerParams(
            collective_id=0, has_side_effects=True, vmem_limit_bytes=56 * 2**20
        ),
        cost_estimate=pl.CostEstimate(flops=6 * TILE * TILE * WIDTH, bytes_accessed=2**20, transcendentals=2 * TILE * TILE),
        name="pairs",
    )(images, texts, log_scale, bias.reshape(1, 1))
    return pl.pallas_call(
        finish,
        out_shape=(grad, grad, scalar, scalar, scalar),
        in_specs=[vmem] * 6,
        out_specs=(vmem, vmem, smem, smem, smem),
        name="finish",
    )(images, texts, image_sum, text_sum, stat_sum, log_scale)


def solution(mesh):
    rows = P(("row", "col"), None)
    return jax.shard_map(
        body,
        mesh=mesh,
        in_specs=(rows, rows, P(), P()),
        out_specs=(rows, rows, P(), P(), P()),
        check_vma=False,
    )
```

```python
import jax
import jax.numpy as jnp
from jax import lax
from jax.experimental import pallas as pl
from jax.experimental.pallas import tpu as pltpu
from jax.sharding import PartitionSpec as P

MESH = pl.DeviceIdType.MESH
F32 = jnp.float32
BF16 = jnp.bfloat16
ROWS = 64
QUARTER = 16
HALF = 32
WIDTH = 1152
PAIRS = 16384
LOG2E = 1.4426950408889634
TILE = 1024

GATHER_PARTS = (
    ((0, 1),),
    ((0, 1), (1, 2)),
    ((0, 1), (1, 2), (2, 4)),
    ((0, 1), (1, 2), (2, 4), (4, 6), (6, 8)),
)
REDUCE_PARTS = (
    ((1, 2),),
    ((3, 4), (2, 3)),
    ((6, 8), (5, 6), (4, 5)),
    ((12, 16), (10, 12), (9, 10), (8, 9)),
)
FIRST_PART = (0, 1, 3, 6)
UP = {0: 0, 1: 2, 2: 4, 3: 6, 4: 7}
DOWN = {0: 0, 1: 1, 2: 3, 3: 5, 4: 7}


def unit_rows(raw):
    values = raw[...].astype(F32)
    inverse = lax.rsqrt(jnp.sum(values * values, axis=1, keepdims=True) + 1e-06)
    return values * inverse, inverse


def encode(v):
    squared = v * v
    return (v * jnp.abs(v) * squared).astype(BF16)


def decode(y):
    y = y.astype(F32)
    inverse = lax.rsqrt(jnp.maximum(jnp.abs(y), 1e-37))
    return y * inverse * inverse * lax.rsqrt(inverse)


def kernel(
    images_in, texts_in, log_scale, bias,
    image_sum, text_sum, stat_sum,
    img, txt, w, iacc, tacc, isend, irecv, csend, crecv, tsend, trecv, stat, acc,
    gi_s, gi_r, gt_s, gt_r, gc_s, gc_r, ri_s, ri_r, rc_s, rc_r, rt_s, rt_r, st_s, st_r, images, texts, in_s,
):
    row = lax.axis_index("row")
    col = lax.axis_index("col")
    x = 2 * (col // 4) + (row // 2) % 2
    y = col % 4
    z = row // 4
    core = row % 2

    def device(x, y, z, core):
        return (z * 4 + (x % 2) * 2 + core, (x // 2) * 4 + y)

    x_flip = x + 1 - 2 * (x % 2)
    y_flip = y + 1 - 2 * (y % 2)
    plane = (
        device(x_flip, y, z, core),
        device(x, y_flip, z, core),
        device(3 - x, y, z, core),
        device(x, 3 - y, z, core),
    )
    above = device(x, y, (z + 1) % 8, core)
    below = device(x, y, (z + 7) % 8, core)
    sibling = device(x, y, z, 1 - core)

    barrier = pltpu.get_barrier_semaphore()
    for other in (*plane, above, below, sibling):
        pl.semaphore_signal(barrier, inc=1, device_id=other, device_id_type=MESH)

    inputs = [
        pltpu.make_async_copy(src, dst, in_s.at[i])
        for i, (src, dst) in enumerate(((images_in, images), (texts_in, texts)))
    ]
    for c in inputs:
        c.start()

    def copy(src, dst, send, recv, to):
        return pltpu.make_async_remote_copy(
            src_ref=src, dst_ref=dst, send_sem=send, recv_sem=recv, device_id=to, device_id_type=MESH
        )

    def start(c):
        c.start()

    def gather_image(q, s, part):
        a, b = GATHER_PARTS[s][part]
        n = FIRST_PART[s] + part
        return copy(
            img.at[a:b, q], img.at[2**s + a : 2**s + b, q], gi_s, gi_r.at[n], plane[(q + s) % 4]
        )

    def gather_text(way, step, half):
        slots = (UP, DOWN)[way]
        src, dst = slots[step], slots[step + 1]
        rows = slice(half * HALF, (half + 1) * HALF)
        return copy(
            txt.at[src, 0, rows], txt.at[dst, 0, rows],
            gt_s, gt_r.at[way, step, half], (above, below)[way],
        )

    def share_text(slot, half):
        rows = slice(half * HALF, (half + 1) * HALF)
        return copy(txt.at[slot, 0, rows], txt.at[slot, 1, rows], gc_s, gc_r.at[slot, half], sibling)

    def reduce_image(q, s, part):
        a, b = REDUCE_PARTS[s][part]
        n = FIRST_PART[s] + part
        return copy(isend.at[a:b, q], irecv.at[a:b, q], ri_s, ri_r.at[n], plane[(q + s) % 4])

    def share_sum(slot):
        return copy(csend.at[slot], crecv.at[slot], rc_s, rc_r.at[slot], sibling)

    def reduce_text(way, m, half):
        rows = slice(half * HALF, (half + 1) * HALF)
        return copy(
            tsend.at[way, m, rows], trecv.at[way, m, rows],
            rt_s, rt_r.at[way, m, half], (above, below)[way],
        )

    def send_stat(n, src, to):
        return copy(stat.at[src], stat.at[n], st_s, st_r.at[n // 16], to)

    inputs[0].wait()
    img[0] = unit_rows(images)[0].astype(BF16).reshape(4, QUARTER, WIDTH)
    inputs[1].wait()
    txt[0, 0] = unit_rows(texts)[0].astype(BF16)
    scale = jnp.exp(log_scale[...])
    shift = bias[...]
    scale_two = scale * LOG2E
    shift_two = shift * LOG2E
    acc[...] = jnp.zeros_like(acc)
    pl.semaphore_wait(barrier, 7)

    def block(first_row, rows, first_col, columns):
        c = lax.dot_general(
            img[pl.ds(first_row // 64, rows // 64)].reshape(rows, WIDTH),
            txt[first_col // 128 : (first_col + columns) // 128].reshape(columns, WIDTH),
            (((1,), (1,)), ((), ())),
            preferred_element_type=F32,
        )
        e = jnp.exp2(c * scale_two + shift_two)
        gate = e / (1.0 + e)
        w[pl.ds(first_row, rows), first_col : first_col + columns] = (scale * gate).astype(BF16)

        def fold(v):
            v = jnp.sum(v.reshape(-1, 16, columns), axis=0)
            return sum(v[:, k : k + 128] for k in range(0, columns, 128))

        fourth = rows // 4
        a, b = e[: 2 * fourth], e[2 * fourth :]
        a = a + b + a * b
        a, b = a[:fourth], a[fourth:]
        acc[0] = acc[0] + fold(jnp.log1p(a + b + a * b))
        acc[1] = acc[1] + fold(gate * c)
        acc[2] = acc[2] + fold(gate)

    def blocks(first_slot, end_slot, first_text, end_text):
        def one(i, _):
            block(pl.multiple_of(first_slot * 64 + i * 256, 256), 256, first_text * 128, (end_text - first_text) * 128)
            return 0

        lax.fori_loop(0, (end_slot - first_slot) // 4, one, 0)

    def own_pairs():
        c = lax.dot_general(
            img[0].reshape(ROWS, WIDTH),
            txt[0].reshape(2 * ROWS, WIDTH),
            (((1,), (1,)), ((), ())),
            preferred_element_type=F32,
        )
        logit = scale * c + shift
        same = lax.broadcasted_iota(jnp.int32, (ROWS, 128), 0) == lax.broadcasted_iota(jnp.int32, (ROWS, 128), 1)
        match = -scale / (1.0 + jnp.exp(logit))
        w[:ROWS, :128] = jnp.where(same, match, w[:ROWS, :128].astype(F32)).astype(BF16)
        for k, v in enumerate((logit, c, jnp.ones_like(c))):
            acc[k] = acc[k] - jnp.where(same, v, 0.0).reshape(4, 16, 128).sum(axis=0)

    for s in range(4):
        for q in range(4):
            start(gather_image(q, s, 0))
        if s < 2:
            for way in range(2):
                start(gather_text(way, 0, s if way == 0 else 1 - s))
    for half in range(2):
        start(share_text(0, half))

    def pass_text(way, step, half):
        gather_text(way, step, half).wait_recv()
        slot = (UP, DOWN)[way][step + 1]
        if step < 2 or (step == 2 and half == way):
            start(gather_text(way, step + 1, half))
        start(share_text(slot, half))

    def got_image(s, part):
        a, b = GATHER_PARTS[s][part]
        all_four = img.at[2**s + a : 2**s + b]
        copy(all_four, all_four, gi_s, gi_r.at[FIRST_PART[s] + part], sibling).wait_recv()

    def pass_image(stages, part):
        for s in stages:
            for q in range(4):
                start(gather_image(q, s, part))

    def got_shared(slots):
        for slot in slots:
            for half in range(2):
                share_text(slot, half).wait_recv()

    got_image(0, 0)
    pass_image((1, 2, 3), 1)
    for way in range(2):
        pass_text(way, 0, way)
    for way in range(2):
        pass_text(way, 0, 1 - way)
    got_image(1, 0)
    got_image(1, 1)
    pass_image((2, 3), 2)
    got_shared((0, 1, 2))
    blocks(0, 4, 0, 3)
    own_pairs()
    for way in range(2):
        pass_text(way, 1, way)
    for way in range(2):
        pass_text(way, 1, 1 - way)
    for part in range(3):
        got_image(2, part)
    pass_image((3,), 3)
    pass_image((3,), 4)
    blocks(4, 8, 0, 3)
    got_shared((3, 4))
    for way in range(2):
        pass_text(way, 2, way)
    blocks(0, 8, 3, 5)
    for part in range(3):
        got_image(3, part)
    for way in range(2):
        pass_text(way, 2, 1 - way)
    blocks(8, 12, 0, 5)
    got_shared((5, 6))
    blocks(0, 4, 5, 7)
    for way in range(2):
        pass_text(way, 3, way)
    blocks(4, 12, 5, 7)
    got_image(3, 3)
    block(12 * ROWS, 128, 0, 896)
    got_image(3, 4)
    block(14 * ROWS, 128, 0, 896)
    got_shared((7,))
    block(0, TILE, 896, 128)

    def stat_plane(n):
        return send_stat(n, 0, device((x + n // 4) % 4, (y + n % 4) % 4, z, core))

    def stat_column(n):
        return send_stat(16 + n, 16, device(x, y, (z + n // 2) % 8, (core + n) % 2))

    def stat_own():
        stat[0] = jnp.zeros((8, 128), F32)
        for k in range(3):
            stat[0, k : k + 1] = jnp.sum(acc[k], axis=0, keepdims=True)
        for n in range(1, 16):
            start(stat_plane(n))

    def stat_turn():
        copy(stat.at[1:16], stat.at[1:16], st_s, st_r.at[0], sibling).wait_recv()
        total = stat[0]
        for n in range(1, 16):
            total = total + stat[n]
        stat[16] = total
        for n in range(1, 16):
            start(stat_column(n))

    def stat_last():
        copy(stat.at[17:32], stat.at[17:32], st_s, st_r.at[1], sibling).wait_recv()
        total = stat[16]
        for n in range(17, 32):
            total = total + stat[n]
        stat_sum[...] = total

    def image_part(slot):
        return jnp.dot(
            w[slot * 64 : (slot + 4) * 64, :], txt[...].reshape(TILE, WIDTH), preferred_element_type=F32
        ).reshape(4, 4, QUARTER, WIDTH)

    def text_part(slot, count):
        part = lax.dot_general(
            w[:, slot * 128 : (slot + count) * 128],
            img[...].reshape(TILE, WIDTH),
            (((0,), (0,)), ((), ())),
            preferred_element_type=F32,
        ).reshape(count, 2, ROWS, WIDTH)
        csend[slot : slot + count] = encode(part[:, 1])
        tacc[slot : slot + count] = part[:, 0]
        for k in range(slot, slot + count):
            start(share_sum(k))

    def send_images(s, parts):
        for part in parts:
            for q in range(4):
                start(reduce_image(q, s, part))

    def wait_images(s, part):
        a, b = REDUCE_PARTS[s][part]
        copy(isend.at[a:b], irecv.at[a:b], ri_s, ri_r.at[FIRST_PART[s] + part], sibling).wait_recv()

    def add_images(first, count, stage, forward):
        def one(i, _):
            slot = first + i
            total = iacc[slot] + decode(irecv[2**stage + slot])
            if forward:
                isend[slot] = encode(total)
            else:
                iacc[slot] = total
            return 0

        lax.fori_loop(0, count, one, 0)

    def join_texts(slot):
        share_sum(slot).wait_recv()
        tacc[slot] = tacc[slot] + decode(crecv[slot])

    def pass_sum(way, m, half):
        slot = (DOWN, UP)[way][m]
        arrives = m == 3 and half == way or m < 3
        if arrives:
            reduce_text(way, m + 1, half).wait_recv()
        rows = slice(half * HALF, (half + 1) * HALF)
        total = tacc[slot, rows]
        if arrives:
            total = total + decode(trecv[way, m + 1, rows])
        tsend[way, m, rows] = encode(total)
        start(reduce_text(way, m, half))

    def pass_sums(m, own):
        for way in range(2):
            pass_sum(way, m, way if own else 1 - way)

    isend[12:16] = encode(image_part(12))
    send_images(3, (0,))
    text_part(7, 1)
    text_part(5, 2)
    join_texts(7)
    pass_sums(4, True)
    stat_own()
    isend[8:12] = encode(image_part(8))
    send_images(3, (1, 2, 3))
    join_texts(5)
    join_texts(6)
    pass_sums(3, False)
    text_part(3, 2)
    pass_sums(3, True)
    wait_images(3, 0)
    isend[4:8] = encode(image_part(4) + decode(irecv[12:16]))
    send_images(2, (0, 1, 2))
    join_texts(3)
    join_texts(4)
    pass_sums(2, False)
    stat_turn()
    text_part(0, 3)
    pass_sums(2, True)
    for part in (1, 2, 3):
        wait_images(3, part)
    iacc[0:4] = image_part(0) + decode(irecv[8:12])
    wait_images(2, 0)
    add_images(3, 1, 2, True)
    send_images(1, (0,))
    add_images(2, 1, 2, True)
    send_images(1, (1,))
    join_texts(1)
    join_texts(2)
    pass_sums(1, False)
    join_texts(0)
    wait_images(2, 1)
    wait_images(2, 2)
    add_images(0, 2, 2, False)
    pass_sums(1, True)
    wait_images(1, 0)
    add_images(1, 1, 1, True)
    send_images(0, (0,))
    wait_images(1, 1)
    add_images(0, 1, 1, False)
    stat_last()

    for way in range(2):
        for half in range(2):
            reduce_text(way, 1, half).wait_recv()
    text_sum[...] = tacc[0] + decode(trecv[0, 1]) + decode(trecv[1, 1])
    wait_images(0, 0)
    image_sum[...] = (iacc[0] + decode(irecv[1])).reshape(ROWS, WIDTH)
    for view, sem in (
        (img.at[0:15], gi_s),
        (txt.at[0:7, 0], gt_s),
        (txt.at[0:8, 0], gc_s),
        (isend.at[1:16], ri_s),
        (csend.at[0:8], rc_s),
        (csend.at[0:7], rt_s),
        (stat.at[0:30], st_s),
    ):
        copy(view, view, sem, in_s.at[0], sibling).wait_send()


def finish(images, texts, image_sum, text_sum, stat_sum, log_scale, image_grad, text_grad, loss, scale_grad, bias_grad):
    for raw, total, out in ((images, image_sum, image_grad), (texts, text_sum, text_grad)):
        unit, inverse = unit_rows(raw)
        grad = total[...] * (1.0 / PAIRS)
        out[...] = inverse * (grad - unit * jnp.sum(unit * grad, axis=1, keepdims=True))
    scale = jnp.exp(jnp.broadcast_to(log_scale[...], (1, 128)))
    loss[0] = jnp.sum(stat_sum[0:1]) * (1.0 / PAIRS)
    scale_grad[0] = jnp.sum(stat_sum[1:2] * scale) * (1.0 / PAIRS)
    bias_grad[0] = jnp.sum(stat_sum[2:3]) * (1.0 / PAIRS)


def body(images, texts, log_scale, bias):
    vmem = pl.BlockSpec(memory_space=pltpu.VMEM)
    smem = pl.BlockSpec(memory_space=pltpu.SMEM)
    dma = pltpu.SemaphoreType.DMA
    grad = jax.ShapeDtypeStruct((ROWS, WIDTH), F32)
    scalar = jax.ShapeDtypeStruct((1,), F32)
    log_scale = log_scale.reshape(1, 1)
    image_sum, text_sum, stat_sum = pl.pallas_call(
        kernel,
        out_shape=(grad, grad, jax.ShapeDtypeStruct((8, 128), F32)),
        in_specs=[pl.BlockSpec(memory_space=pl.ANY)] * 2 + [vmem] * 2,
        out_specs=(vmem,) * 3,
        scratch_shapes=[
            pltpu.VMEM((16, 4, QUARTER, WIDTH), BF16),
            pltpu.VMEM((8, 2, ROWS, WIDTH), BF16),
            pltpu.VMEM((TILE, TILE), BF16),
            pltpu.VMEM((8, 4, QUARTER, WIDTH), F32),
            pltpu.VMEM((8, ROWS, WIDTH), F32),
            pltpu.VMEM((16, 4, QUARTER, WIDTH), BF16),
            pltpu.VMEM((16, 4, QUARTER, WIDTH), BF16),
            pltpu.VMEM((8, ROWS, WIDTH), BF16),
            pltpu.VMEM((8, ROWS, WIDTH), BF16),
            pltpu.VMEM((2, 5, ROWS, WIDTH), BF16),
            pltpu.VMEM((2, 5, ROWS, WIDTH), BF16),
            pltpu.VMEM((33, 8, 128), F32),
            pltpu.VMEM((3, 16, 128), F32),
            dma(()), dma((11,)),
            dma(()), dma((2, 4, 2)),
            dma(()), dma((8, 2)),
            dma(()), dma((10,)),
            dma(()), dma((8,)),
            dma(()), dma((2, 5, 2)),
            dma(()), dma((2,)),
            pltpu.VMEM((ROWS, WIDTH), BF16), pltpu.VMEM((ROWS, WIDTH), BF16), dma((2,)),
        ],
        compiler_params=pltpu.CompilerParams(
            collective_id=0, has_side_effects=True, vmem_limit_bytes=56 * 2**20
        ),
        cost_estimate=pl.CostEstimate(flops=6 * TILE * TILE * WIDTH, bytes_accessed=2**20, transcendentals=2 * TILE * TILE),
        name="pairs",
    )(images, texts, log_scale, bias.reshape(1, 1))
    return pl.pallas_call(
        finish,
        out_shape=(grad, grad, scalar, scalar, scalar),
        in_specs=[vmem] * 6,
        out_specs=(vmem, vmem, smem, smem, smem),
        name="finish",
    )(images, texts, image_sum, text_sum, stat_sum, log_scale)


def solution(mesh):
    rows = P(("row", "col"), None)
    return jax.shard_map(
        body,
        mesh=mesh,
        in_specs=(rows, rows, P(), P()),
        out_specs=(rows, rows, P(), P(), P()),
        check_vma=False,
    )
```
